128 devices in a mesh: src: 4 (over z_hi, core), tgt: 32 (over y, z_lo, x).
Axes of the slice: x: 4, y: 4, z: 4 (z_hi: 2, z_lo: 2; z = z_hi * 2 + z_lo), core: 2. Of those that a mesh axis runs over, the one named last changes fastest.
Arguments:
- forward_init: float32 [256, 32768], P(None, 'src'), may hold values from 0.1 to 10
- transition: bfloat16 [32768, 32768], P('src', 'tgt'), may hold values from 0 to 2976, as said below
- emission: bfloat16 [4096, 32768], P('src', 'tgt'), may hold values from 0.25 to 4
- tokens: int32 [3, 256], replicated, may hold values from 0 to 4095
Outputs:
- forward: float32 [256, 32768], P('src', 'tgt')
- log_total: float32 [256], P('src')
The draws below stay inside these ranges and needn't reach their ends.
Inputs may be any that keep to these rules, and one draw needn't show every extreme that they name: `transition`: every weight is positive.
All inputs are finite; a program needn't handle non-finite values.
Results may differ from the reference program's by a relative error of at most 0.00082.
Values may be sent and summed in bfloat16 or wider, within the bound.
A program may use at most 128 MiB of HBM per device.

```python
import math
import jax
import jax.numpy as jnp
from jax import lax

S = 32768
V = 4096
SEQS = 256
STEPS = 3


def draw_transition(key, part):
    key = jax.random.fold_in(key, 7)
    normal = jax.random.normal(key, (S, S), jnp.float32)
    return jnp.exp(4.0 * jnp.clip(normal, -4.0, 4.0) - 8.0).astype(jnp.bfloat16)


def set_ends(values, rng, least, top_value):
    dims = values.shape
    spot = [jax.random.randint(jax.random.fold_in(rng, axis), (), 0, dims[axis]) for axis in range(len(dims))]
    values = values.at[tuple(spot)].set(least)
    longest = dims.index(max(dims))
    spot[longest] = (spot[longest] + 1) % dims[longest]
    return values.at[tuple(spot)].set(top_value)


def shard_levels(rng, dims, split, smallest, largest):
    def one(axis_at, parts):
        draws = jax.random.uniform(jax.random.fold_in(jax.random.fold_in(rng, 6), axis_at), (parts,), jnp.float32, smallest / len(split), largest / len(split))
        return jnp.repeat(jnp.exp(draws), dims[axis_at] // parts).reshape((-1,) + (1,) * (len(dims) - axis_at - 1))

    gain = one(*split[0])
    for cut in split[1:]:
        gain = gain * one(*cut)
    return gain


def setup_inputs(seed: int = 0) -> dict:
    key_list = jax.random.split(jax.random.key(seed), 5)
    forward_init = jnp.clip(jnp.exp(math.log(10.0) - 4.6051702 * jax.random.uniform(key_list[0], (SEQS, S), jnp.float32) ** shard_levels(key_list[0], (SEQS, S), ((1, 4),), -0.2, 0.2)), 0.1, 10.0)
    transition = draw_transition(jax.random.fold_in(key_list[4], 71), 0)
    emission = jnp.clip(jnp.exp(math.log(4.0) - 2.7725887 * jax.random.uniform(key_list[2], (V, S), jnp.float32) ** shard_levels(key_list[2], (V, S), ((0, 4), (1, 32)), -0.2, 0.2)), 0.25, 4.0).astype(jnp.bfloat16)
    tokens = set_ends(jax.random.randint(key_list[3], (STEPS, SEQS), 0, V), jax.random.fold_in(key_list[3], 1), 0, V - 1).astype(jnp.int32)
    return {"forward_init": forward_init, "transition": transition, "emission": emission, "tokens": tokens}


def reference(forward_init, transition, emission, tokens):
    width = min(S, 4096)
    count = S // width
    current = forward_init.astype(jnp.bfloat16)
    log_sum = jnp.zeros((SEQS,), jnp.float32)
    normed = forward_init
    for step in range(STEPS):
        left = current.astype(jnp.float32)

        def column_block(index):
            piece = lax.dynamic_slice_in_dim(transition, index * width, width, 1).astype(jnp.float32)
            return jnp.dot(left, piece, precision=lax.Precision.HIGHEST)

        blocks = lax.map(column_block, jnp.arange(count, dtype=jnp.int32))
        carried = jnp.transpose(blocks, (1, 0, 2)).reshape(SEQS, S)
        rows = jnp.take(emission, tokens[step], axis=0).astype(jnp.float32)
        fresh = carried * rows / S
        total = jnp.sum(fresh, axis=1) / S
        log_sum = log_sum + jnp.log(total)
        normed = fresh / total[:, None]
        current = normed.astype(jnp.bfloat16)
    return normed, log_sum
```

```python
import functools

import jax
import jax.numpy as jnp
from jax import lax
from jax.experimental import pallas as pl
from jax.experimental.pallas import tpu as pltpu
from jax.sharding import PartitionSpec as P

MESH = pl.DeviceIdType.MESH
BLK = 1024
KB = 8
HALVES = 1
R = 64 // HALVES
ROWS = 4 * R
CA = 640
STEPS = 3
S = 32768.0


def place(q):
    return (q % 2) * 2 + q // 2


def kernel(tok, fwd, trans, emis, out, logs, tbuf, ebuf, stage, cur, acc, rs1, mid, rs2, erow, er1, emid, er2, emine, blk, tota, totb, fresh, lsum,
           ld_t, ld_f, ld_e, d_s, d_r, z_s, z_r, ed_s, ed_r, ez_s, ez_r, a_s, a_r, b_s, b_r, pa_s, pa_r, pb_s, pb_r, xa_s, xa_r, yb_s, yb_r, loc):
    s = lax.axis_index("src")
    t = lax.axis_index("tgt")
    zh, c = s // 2, s % 2
    y, zl, x = t // 8, (t // 4) % 2, t % 4
    is_self = s == y

    def dev(s_, y_, zl_, x_):
        return (s_, y_ * 8 + zl_ * 4 + x_)

    core = dev(zh * 2 + 1 - c, y, zl, x)
    zhp = dev((1 - zh) * 2 + c, y, zl, x)
    plane = [(dz, dx) for dz in range(2) for dx in range(4)]

    def in_plane(dz, dx):
        return dev(s, y, (zl + dz) % 2, (x + dx) % 4)

    def in_y(dy):
        return dev(s, (y + dy) % 4, zl, x)

    spread = [(o, dz) for dz in range(2) for o in range(4)]

    def dest_a(o, dz):
        return dev(y, (y + o) % 4, (zl + dz) % 2, x)

    def dest_b(o, dz):
        return dev(y, s, (zl + dz) % 2, (x + o) % 4)

    e_ld = pltpu.make_async_copy(emis, ebuf, ld_e)
    e_ld.start()

    def kb_rows(i):
        return pl.ds(pl.multiple_of(((i % 2) * 4 + i // 2) * BLK, BLK), BLK)

    def f_ld(i, slot):
        return pltpu.make_async_copy(fwd.at[:, kb_rows(i)], stage.at[slot], ld_f.at[slot])

    def t_ld(i):
        return pltpu.make_async_copy(trans.at[kb_rows(i)], tbuf.at[i], ld_t.at[i])

    for i in range(KB):
        if i < 2:
            f_ld(i, i).start()
        t_ld(i).start()

    barrier = pltpu.get_barrier_semaphore()

    def hello(d):
        pl.semaphore_signal(barrier, inc=1, device_id=d, device_id_type=MESH)

    hello(core)
    hello(zhp)
    n = 2
    for dz, dx in plane[1:]:
        hello(in_plane(dz, dx))
        n += 1
    for dy in range(1, 4):
        hello(in_y(dy))
        n += 1
    for o, dz in spread:
        src_a = dev((y + o) % 4, s, (zl + dz) % 2, x)
        src_b = dev(y, s, (zl + dz) % 2, (x + o) % 4)
        if (o, dz) == (0, 0):
            @pl.when(jnp.logical_not(is_self))
            def _():
                hello(src_a)
                hello(src_b)
        else:
            hello(src_a)
            hello(src_b)
            n += 2
    @pl.when(is_self)
    def _():
        pl.semaphore_wait(barrier, n)

    @pl.when(jnp.logical_not(is_self))
    def _():
        pl.semaphore_wait(barrier, n + 2)

    def remote(src, dst, ss, rs, d):
        return pltpu.make_async_remote_copy(src_ref=src, dst_ref=dst, send_sem=ss, recv_sem=rs, device_id=d, device_id_type=MESH)

    e_ld.wait()
    ecopies = []
    for k in range(STEPS):
        def pick(p, _):
            rows = pl.ds(pl.multiple_of(k * 256 + p * 64, 64), 64)
            ids = tok[rows, :]
            hot = jnp.concatenate(
                [jnp.where(ids == lax.broadcasted_iota(jnp.int32, (64, 128), 1) + v * 128, 1.0, 0.0) for v in range(8)], axis=1
            ).astype(jnp.bfloat16)
            erow[rows, :] = jnp.dot(hot, ebuf[...], preferred_element_type=jnp.float32).astype(jnp.bfloat16)
            return 0

        lax.fori_loop(0, 4, pick, 0)
        cp = remote(erow.at[pl.ds(pl.multiple_of(k * 256 + (1 - c) * 128, 128), 128)], er1.at[k], ed_s.at[k], ed_r.at[k], core)
        cp.start()
        ecopies.append(cp)

    ez = []
    for k in range(STEPS):
        ecopies[k].wait_recv()
        other = pl.multiple_of((1 - zh) * 64, 64)
        emid[k] = erow[pl.ds(pl.multiple_of(k * 256 + c * 128 + (1 - zh) * 64, 64), 64), :] + er1[k, pl.ds(other, 64), :]
        cp = remote(emid.at[k], er2.at[k], ez_s.at[k], ez_r.at[k], zhp)
        cp.start()
        ez.append(cp)
        ecopies.append(cp)
        emine[k] = erow[pl.ds(pl.multiple_of(k * 256 + c * 128 + zh * 64, 64), 64), :] + er1[k, pl.ds(pl.multiple_of(zh * 64, 64), 64), :]

    for i in range(KB):
        slot = i % 2
        f_ld(i, slot).wait()
        for q in range(4):
            for h in range(HALVES):
                cur[0, h, i, place(q) * R : (place(q) + 1) * R, :] = stage[slot, q * 64 + h * R : q * 64 + (h + 1) * R, :].astype(jnp.bfloat16)
        if i + 2 < KB:
            f_ld(i + 2, slot).start()
        t_ld(i).wait()
        for h in range(HALVES):
            part = jnp.dot(cur[0, h, i], tbuf[i], preferred_element_type=jnp.float32)
            if i == 0:
                acc[0, h] = part
            else:
                acc[0, h] += part

    drain = []

    def product(k, h):
        acc[k, h] = jnp.dot(cur[k, h, 0], tbuf[0], preferred_element_type=jnp.float32)

        def body(i, _):
            acc[k, h] += jnp.dot(cur[k, h, i], tbuf[i], preferred_element_type=jnp.float32)
            return 0

        lax.fori_loop(1, KB, body, 0)

    st = {}

    def core_start(k, h):
        cp = remote(acc.at[k, h, pl.ds(pl.multiple_of((1 - c) * 2 * R, 2 * R), 2 * R)], rs1.at[k, h], d_s.at[k, h], d_r.at[k, h], core)
        cp.start()
        st["d", k, h] = cp
        drain.append(cp)

    def core_end(k, h):
        st["d", k, h].wait_recv()
        mid[k, h] = acc[k, h, pl.ds(pl.multiple_of((c * 2 + 1 - zh) * R, R), R), :] + rs1[k, h, pl.ds(pl.multiple_of((1 - zh) * R, R), R), :]
        cp = remote(mid.at[k, h], rs2.at[k, h], z_s.at[k, h], z_r.at[k, h], zhp)
        cp.start()
        st["z", k, h] = cp
        drain.append(cp)
        fresh[h] = acc[k, h, pl.ds(pl.multiple_of((c * 2 + zh) * R, R), R), :] + rs1[k, h, pl.ds(pl.multiple_of(zh * R, R), R), :]

    def z_end(k, h):
        if h == 0:
            ez[k].wait_recv()
        st["z", k, h].wait_recv()
        rows = pl.ds(h * R, R)
        e = emine[k, rows, :].astype(jnp.float32) + er2[k, rows, :].astype(jnp.float32)
        v = (fresh[h] + rs2[k, h]) * e * (1.0 / S)
        fresh[h] = v
        lanes = v[:, 0:128]
        for g in range(1, 8):
            lanes = lanes + v[:, g * 128 : (g + 1) * 128]
        own = zl * 4 + x
        tota[k, h, own] = lanes
        for j, (dz, dx) in enumerate(plane[1:]):
            cp = remote(tota.at[k, h, own], tota.at[k, h, own], a_s.at[k, h, j], a_r.at[k, h], in_plane(dz, dx))
            cp.start()
            drain.append(cp)

    def a_end(k, h):
        pltpu.make_async_copy(tota.at[k, h, pl.ds(0, 7)], tota.at[k, h, pl.ds(0, 7)], a_r.at[k, h]).wait()
        v = tota[k, h, 0]
        for j in range(1, 8):
            v = v + tota[k, h, j]
        totb[k, h, y] = v
        for j in range(3):
            cp = remote(totb.at[k, h, y], totb.at[k, h, y], b_s.at[k, h, j], b_r.at[k, h], in_y(j + 1))
            cp.start()
            drain.append(cp)

    def b_end(k, h):
        pltpu.make_async_copy(totb.at[k, h, pl.ds(0, 3)], totb.at[k, h, pl.ds(0, 3)], b_r.at[k, h]).wait()
        v = totb[k, h, 0]
        for j in range(1, 4):
            v = v + totb[k, h, j]
        total = jnp.sum(v, axis=1, keepdims=True) * (1.0 / S)
        lg = jnp.broadcast_to(jnp.log(total), (R, 128))
        lsum[h] = lg if k == 0 else lsum[h] + lg
        normed = fresh[h] / total
        if k + 1 == STEPS:
            out[h * R : (h + 1) * R, :] = normed
            logs[h * R : (h + 1) * R, :] = lsum[h]
            return
        blk[k, h] = normed.astype(jnp.bfloat16)
        mine = pl.ds(pl.multiple_of(place(s) * R, R), R)
        home = x * 2 + zl
        for j, (o, dz) in enumerate(spread):
            for half, dest, ss, rs, cols in (
                (0, dest_a(o, dz), pa_s, pa_r, pl.ds(0, CA)),
                (1, dest_b(o, dz), pb_s, pb_r, pl.ds(CA, BLK - CA)),
            ):
                src = blk.at[k, h, :, cols]
                dst = cur.at[k + 1, h, home, mine, cols]
                cp = remote(src, dst, ss.at[k, h, j], rs.at[k, h], dest)
                if (o, dz) == (0, 0):
                    lcp = pltpu.make_async_copy(src, dst, rs.at[k, h])

                    @pl.when(is_self)
                    def _(lcp=lcp):
                        lcp.start()

                    @pl.when(jnp.logical_not(is_self))
                    def _(cp=cp):
                        cp.start()

                    st["self", k, h, half] = cp
                else:
                    cp.start()
                    drain.append(cp)

    def piece_a(k, h, xx, z):
        return cur.at[k + 1, h, xx * 2 + z, :, pl.ds(0, CA)]

    def piece_b(k, h, yy, z):
        return cur.at[k + 1, h, pl.ds(z * 4, 4), pl.ds(pl.multiple_of(place(yy) * R, R), R), pl.ds(CA, BLK - CA)]

    def ring_dev(axis, d):
        return dev(s, y, zl, (x + d + 4) % 4) if axis == 0 else dev(s, (y + d + 4) % 4, zl, x)

    def ring_start(k, h, axis):
        if axis == 0:
            whole = cur.at[k + 1, h, pl.ds(x * 2, 2), :, pl.ds(0, CA)]
            pltpu.make_async_copy(whole, whole, pa_r.at[k, h]).wait()
        else:
            whole = cur.at[k + 1, h, :, pl.ds(pl.multiple_of(place(y) * R, R), R), pl.ds(CA, BLK - CA)]
            pltpu.make_async_copy(whole, whole, pb_r.at[k, h]).wait()
        piece, me = (piece_a, x) if axis == 0 else (piece_b, y)
        ss, rs = (xa_s, xa_r) if axis == 0 else (yb_s, yb_r)
        for j, (d, z) in enumerate(((1, 0), (-1, 1), (1, 1), (-1, 0))):
            p = piece(k, h, me, z)
            cp = remote(p, p, ss.at[k, h, j], rs.at[k, h, j], ring_dev(axis, d))
            cp.start()
            st["r", k, h, axis, j] = cp
            drain.append(cp)

    def ring_pass(k, h, axis):
        piece, me = (piece_a, x) if axis == 0 else (piece_b, y)
        ss, rs = (xa_s, xa_r) if axis == 0 else (yb_s, yb_r)
        for j, (d, z) in ((0, (1, 0)), (1, (-1, 1))):
            st["r", k, h, axis, j].wait_recv()
            p = piece(k, h, (me - d + 4) % 4, z)
            cp = remote(p, p, ss.at[k, h, 4 + j], rs.at[k, h, 4 + j], ring_dev(axis, d))
            cp.start()
            st["r", k, h, axis, 4 + j] = cp
            drain.append(cp)

    def ring_end(k, h, axis):
        for j in range(2, 6):
            st["r", k, h, axis, j].wait_recv()

    hs = range(HALVES)
    for k in range(STEPS):
        if k == 0:
            for h in hs:
                core_start(k, h)
        for h in hs:
            core_end(k, h)
        for h in hs:
            z_end(k, h)
        for h in hs:
            a_end(k, h)
        for h in hs:
            b_end(k, h)
        if k + 1 < STEPS:
            for h in hs:
                for axis in range(2):
                    ring_start(k, h, axis)
                for axis in range(2):
                    ring_pass(k, h, axis)
            for h in hs:
                for axis in range(2):
                    ring_end(k, h, axis)
                product(k + 1, h)
                core_start(k + 1, h)

    for cp in drain:
        cp.wait_send()
    for cp in ecopies:
        cp.wait_send()

    @pl.when(jnp.logical_not(is_self))
    def _():
        for k in range(STEPS - 1):
            for h in hs:
                for half in range(2):
                    st["self", k, h, half].wait_send()


def per_device(forward_init, transition, emission, tokens):
    src = lax.axis_index("src")
    ids = tokens.reshape(STEPS, 2, 2, 64).transpose(0, 2, 1, 3).reshape(STEPS * 256, 1)
    ids = jnp.broadcast_to(ids - src * emission.shape[0], (STEPS * 256, 128))
    hbm = pl.BlockSpec(memory_space=pl.ANY)
    vmem = pl.BlockSpec(memory_space=pltpu.VMEM)
    V = pltpu.VMEM
    D = pltpu.SemaphoreType.DMA
    f32, bf16 = jnp.float32, jnp.bfloat16
    H = HALVES
    out, logs = pl.pallas_call(
        kernel,
        name="forward_window",
        out_shape=(jax.ShapeDtypeStruct((64, BLK), f32), jax.ShapeDtypeStruct((64, 128), f32)),
        in_specs=[vmem, hbm, hbm, hbm],
        out_specs=(vmem, vmem),
        scratch_shapes=[
            V((KB, BLK, BLK), bf16),
            V((1024, BLK), bf16),
            V((2, 256, BLK), f32),
            V((STEPS, H, KB, ROWS, BLK), bf16),
            V((STEPS, H, ROWS, BLK), f32),
            V((STEPS, H, 2 * R, BLK), f32),
            V((STEPS, H, R, BLK), f32),
            V((STEPS, H, R, BLK), f32),
            V((STEPS * 256, BLK), bf16),
            V((STEPS, 128, BLK), bf16),
            V((STEPS, 64, BLK), bf16),
            V((STEPS, 64, BLK), bf16),
            V((STEPS, 64, BLK), bf16),
            V((STEPS - 1, H, R, BLK), bf16),
            V((STEPS, H, 8, R, 128), f32),
            V((STEPS, H, 4, R, 128), f32),
            V((H, R, BLK), f32),
            V((H, R, 128), f32),
            D((KB,)), D((2,)), D,
            D((STEPS, H)), D((STEPS, H)), D((STEPS, H)), D((STEPS, H)),
            D((STEPS,)), D((STEPS,)), D((STEPS,)), D((STEPS,)),
            D((STEPS, H, 7)), D((STEPS, H)), D((STEPS, H, 3)), D((STEPS, H)),
            D((STEPS, H, 8)), D((STEPS, H)), D((STEPS, H, 8)), D((STEPS, H)),
            D((STEPS, H, 6)), D((STEPS, H, 6)), D((STEPS, H, 6)), D((STEPS, H, 6)),
            D,
        ],
        compiler_params=pltpu.CompilerParams(collective_id=0, has_side_effects=True, vmem_limit_bytes=58 * 2**20),
    )(ids, forward_init, transition, emission)
    return out, logs[:, 0]


def solution(mesh):
    placed = (P(None, "src"), P("src", "tgt"), P("src", "tgt"), P())
    return jax.shard_map(
        per_device,
        mesh=mesh,
        in_specs=placed,
        out_specs=(P("src", "tgt"), P("src")),
        check_vma=False,
    )
```

```python
import functools

import jax
import jax.numpy as jnp
from jax import lax
from jax.experimental import pallas as pl
from jax.experimental.pallas import tpu as pltpu
from jax.sharding import PartitionSpec as P

MESH = pl.DeviceIdType.MESH
BLK = 1024
KB = 8
HALVES = 2
R = 64 // HALVES
ROWS = 4 * R
CA = 512
STEPS = 3
AHEAD = 3
S = 32768.0


def place(q):
    return (q % 2) * 2 + q // 2


def kernel(tok, fwd, trans, emis, out, logs, tbuf, ebuf, stage, cur, acc, rs1, mid, rs2, erow, er1, emid, er2, blk, tota, totb, fresh, lsum, col,
           ld_t, ld_f, ld_e, d_s, d_r, z_s, z_r, ed_s, ed_r, ez_s, ez_r, a_s, a_r, b_s, b_r, t_s, t_r, g_s, g_r, xa_s, xa_r, yb_s, yb_r):
    s = lax.axis_index("src")
    t = lax.axis_index("tgt")
    zh, c = s // 2, s % 2
    y, zl, x = t // 8, (t // 4) % 2, t % 4
    is_self = s == y

    def dev(s_, y_, zl_, x_):
        return (s_, y_ * 8 + zl_ * 4 + x_)

    core = dev(zh * 2 + 1 - c, y, zl, x)
    zhp = dev((1 - zh) * 2 + c, y, zl, x)
    plane = [(dh, dz, dx) for dh in range(2) for dz in range(2) for dx in range(4)][1:]

    def in_plane(dh, dz, dx):
        return dev((zh + dh) % 2 * 2 + c, y, (zl + dz) % 2, (x + dx) % 4)

    def in_y(dy):
        return dev(s, (y + dy) % 4, zl, x)

    def in_x(dx):
        return dev(s, y, zl, (x + dx) % 4)

    def turned(dz):
        return dev(y, s, (zl + dz) % 2, x)

    def kb_rows(i):
        return pl.ds(pl.multiple_of(((i % 2) * 4 + i // 2) * BLK, BLK), BLK)

    def f_ld(i):
        return pltpu.make_async_copy(fwd.at[:, kb_rows(i)], stage.at[i], ld_f.at[i])

    def t_ld(i):
        return pltpu.make_async_copy(trans.at[kb_rows(i)], tbuf.at[i], ld_t.at[i])

    e_ld = pltpu.make_async_copy(emis, ebuf, ld_e)
    e_ld.start()

    barrier = pltpu.get_barrier_semaphore()

    def hello(d):
        pl.semaphore_signal(barrier, inc=1, device_id=d, device_id_type=MESH)

    hello(core)
    for p in plane:
        hello(in_plane(*p))
    for dy in range(1, 4):
        hello(in_y(dy))
    hello(turned(1))
    n = 1 + len(plane) + 3 + 1

    @pl.when(jnp.logical_not(is_self))
    def _():
        hello(turned(0))

    for i in range(AHEAD):
        f_ld(i).start()
        t_ld(i).start()

    def remote(src, dst, ss, rs, d):
        return pltpu.make_async_remote_copy(src_ref=src, dst_ref=dst, send_sem=ss, recv_sem=rs, device_id=d, device_id_type=MESH)

    drain = []

    def pick(k):
        ids = jnp.broadcast_to(tok[k : k + 1, :], (128, 256)).T - s * BLK
        ids = jnp.concatenate([ids[q * 64 : (q + 1) * 64, :] for q in (0, 2, 1, 3)], axis=0)
        lane = lax.broadcasted_iota(jnp.int32, (256, 128), 1)
        hot = jnp.concatenate([jnp.where(ids == lane + v * 128, 1.0, 0.0).astype(jnp.bfloat16) for v in range(8)], axis=1)
        erow[k] = jnp.dot(hot, ebuf[...], preferred_element_type=jnp.float32).astype(jnp.bfloat16)

    def own_rows(p, size):
        return pl.ds(pl.multiple_of(p * size, size), size)

    def part_rows(h, p, size):
        return pl.ds(pl.multiple_of(h * ROWS + p * size, size), size)

    est = {}

    def e_core_start(k):
        cp = remote(erow.at[k, own_rows(1 - c, 128)], er1.at[k], ed_s.at[k], ed_r.at[k], core)
        cp.start()
        est["d", k] = cp
        drain.append(cp)

    def e_z_start(k):
        est["d", k].wait_recv()
        for h in range(HALVES):
            for g in range(2):
                emid[k, h, g * R : (g + 1) * R, :] = erow[k, pl.ds(pl.multiple_of(c * 128 + g * 64 + h * R, R), R), :] + er1[k, g * 64 + h * R : g * 64 + (h + 1) * R, :]
            cp = remote(emid.at[k, h], er2.at[k, h], ez_s.at[k, h], ez_r.at[k, h], zhp)
            cp.start()
            est["z", k, h] = cp
            drain.append(cp)

    e_ld.wait()
    pick(0)

    @pl.when(is_self)
    def _():
        pl.semaphore_wait(barrier, n)

    @pl.when(jnp.logical_not(is_self))
    def _():
        pl.semaphore_wait(barrier, n + 1)

    e_core_start(0)
    e_z_start(0)

    acc[0] = jnp.zeros_like(acc[0])

    def first(i, _):
        f_ld(i).wait()
        for q in range(4):
            for h in range(HALVES):
                at = h * ROWS + place(q) * R
                cur[0, i, at : at + R, :] = stage[i, q * 64 + h * R : q * 64 + (h + 1) * R, :].astype(jnp.bfloat16)
        t_ld(i).wait()

        @pl.when(i + AHEAD < KB)
        def _():
            f_ld(i + AHEAD).start()
            t_ld(i + AHEAD).start()

        acc[0] += jnp.dot(cur[0, i], tbuf[i], preferred_element_type=jnp.float32)
        return 0

    lax.fori_loop(0, KB, first, 0)

    def product(k, h):
        def body(j, _):
            cols = pl.ds(pl.multiple_of(j * 512, 512), 512)
            v = jnp.dot(cur[k, 0, h * ROWS : (h + 1) * ROWS, :], tbuf[0, :, cols], preferred_element_type=jnp.float32)
            for i in range(1, KB):
                v = v + jnp.dot(cur[k, i, h * ROWS : (h + 1) * ROWS, :], tbuf[i, :, cols], preferred_element_type=jnp.float32)
            acc[k, h * ROWS : (h + 1) * ROWS, cols] = v
            return 0

        lax.fori_loop(0, BLK // 512, body, 0)

    st = {}

    def core_start(k, h):
        cp = remote(acc.at[k, part_rows(h, 1 - c, 2 * R)], rs1.at[k, h], d_s.at[k, h], d_r.at[k, h], core)
        cp.start()
        st["d", k, h] = cp
        drain.append(cp)

    def emission(k, h, g):
        rows = own_rows(g, R)
        return emid[k, h, rows, :].astype(jnp.float32) + er2[k, h, rows, :].astype(jnp.float32)

    def core_end(k, h):
        st["d", k, h].wait_recv()
        mid[k, h] = acc[k, part_rows(h, c, 2 * R), :] + rs1[k, h]
        est["z", k, h].wait_recv()
        parts = []
        for g in range(2):
            v = mid[k, h, g * R : (g + 1) * R, :] * emission(k, h, g)
            lanes = v[:, 0:128]
            for j in range(1, 8):
                lanes = lanes + v[:, j * 128 : (j + 1) * 128]
            parts.append(lanes)
            if R < 64:
                parts.append(jnp.zeros((64 - R, 128), jnp.float32))
        share = jnp.sum(jnp.concatenate(parts, axis=0).T, axis=0, keepdims=True)
        own = zh * 8 + zl * 4 + x
        tota[k, h, own] = jnp.broadcast_to(share, (8, 128))
        for j, p in enumerate(plane):
            cp = remote(tota.at[k, h, own], tota.at[k, h, own], a_s.at[k, h, j], a_r.at[k, h], in_plane(*p))
            cp.start()
            drain.append(cp)

    def z_start(k, h):
        cp = remote(mid.at[k, h, own_rows(1 - zh, R)], rs2.at[k, h], z_s.at[k, h], z_r.at[k, h], zhp)
        cp.start()
        st["z", k, h] = cp
        drain.append(cp)

    def a_end(k, h):
        pltpu.make_async_copy(tota.at[k, h, pl.ds(0, 15)], tota.at[k, h, pl.ds(0, 15)], a_r.at[k, h]).wait()
        v = tota[k, h, 0]
        for j in range(1, 16):
            v = v + tota[k, h, j]
        totb[k, h, y] = v
        for j in range(3):
            cp = remote(totb.at[k, h, y], totb.at[k, h, y], b_s.at[k, h, j], b_r.at[k, h], in_y(j + 1))
            cp.start()
            drain.append(cp)

    def z_end(k, h):
        st["z", k, h].wait_recv()
        fresh[k, h] = (mid[k, h, own_rows(zh, R), :] + rs2[k, h]) * emission(k, h, zh) * (1.0 / S)

    def b_end(k, h):
        pltpu.make_async_copy(totb.at[k, h, pl.ds(0, 3)], totb.at[k, h, pl.ds(0, 3)], b_r.at[k, h]).wait()
        v = totb[k, h, 0]
        for j in range(1, 4):
            v = v + totb[k, h, j]
        total = v * (1.0 / (S * S))
        col[h] = jnp.broadcast_to(total[0:1, :], (128, 128)).T
        normed = fresh[k, h] / col[h, pl.ds(pl.multiple_of(zh * 64, 64), R), 0:1]
        if k + 1 == STEPS:
            out[h * R : (h + 1) * R, :] = normed
        else:
            blk[k, h] = normed.astype(jnp.bfloat16)
            dst = cur.at[k + 1, x * 2 + zl, part_rows(h, place(s), R)]
            far = remote(blk.at[k, h], dst, t_s.at[k, h, 1], t_r.at[k, h], turned(1))
            far.start()
            drain.append(far)
            near = remote(blk.at[k, h], dst, t_s.at[k, h, 0], t_r.at[k, h], turned(0))
            here = pltpu.make_async_copy(blk.at[k, h], dst, t_r.at[k, h])

            @pl.when(is_self)
            def _():
                here.start()

            @pl.when(jnp.logical_not(is_self))
            def _():
                near.start()

            st["near", k, h] = near
        lsum[h] = jnp.log(total) if k == 0 else lsum[h] + jnp.log(total)

    def gather_start(k, h):
        rows = part_rows(h, place(y), R)
        whole = cur.at[k + 1, pl.ds(x * 2, 2), rows]
        pltpu.make_async_copy(whole, whole, t_r.at[k, h]).wait()
        for j in (0, 2, 1):
            for axis, cols, d in ((0, pl.ds(0, CA), in_y(j + 1)), (1, pl.ds(CA, BLK - CA), in_x(j + 1))):
                p = cur.at[k + 1, pl.ds(x * 2, 2), rows, cols]
                cp = remote(p, p, g_s.at[k, h, axis, j], g_r.at[k, h, axis], d)
                cp.start()
                drain.append(cp)

    def piece_a(k, h, xx, z):
        return cur.at[k + 1, xx * 2 + z, pl.ds(h * ROWS, ROWS), pl.ds(0, CA)]

    def piece_b(k, h, yy, z):
        return cur.at[k + 1, pl.ds(z * 4, 4), part_rows(h, place(yy), R), pl.ds(CA, BLK - CA)]

    def ring_dev(axis, d):
        return in_x(d + 4) if axis == 0 else in_y(d + 4)

    def ring_start(k, h, axis):
        if axis == 0:
            got = cur.at[k + 1, pl.ds(x * 2, 2), pl.ds(h * ROWS, 3 * R), pl.ds(0, CA)]
        else:
            got = cur.at[k + 1, pl.ds(0, 6), part_rows(h, place(y), R), pl.ds(CA, BLK - CA)]
        pltpu.make_async_copy(got, got, g_r.at[k, h, axis]).wait()
        piece, me = (piece_a, x) if axis == 0 else (piece_b, y)
        ss, rs = (xa_s, xa_r) if axis == 0 else (yb_s, yb_r)
        for j, (d, z) in enumerate(((1, 0), (-1, 1), (1, 1), (-1, 0))):
            p = piece(k, h, me, z)
            cp = remote(p, p, ss.at[k, h, j], rs.at[k, h, j], ring_dev(axis, d))
            cp.start()
            st["r", k, h, axis, j] = cp
            drain.append(cp)

    def ring_pass(k, h, axis):
        piece, me = (piece_a, x) if axis == 0 else (piece_b, y)
        ss, rs = (xa_s, xa_r) if axis == 0 else (yb_s, yb_r)
        for j, (d, z) in ((0, (1, 0)), (1, (-1, 1))):
            st["r", k, h, axis, j].wait_recv()
            p = piece(k, h, (me - d + 4) % 4, z)
            cp = remote(p, p, ss.at[k, h, 4 + j], rs.at[k, h, 4 + j], ring_dev(axis, d))
            cp.start()
            st["r", k, h, axis, 4 + j] = cp
            drain.append(cp)

    def ring_end(k, h, axis):
        for j in range(2, 6):
            st["r", k, h, axis, j].wait_recv()

    hs = range(HALVES)

    def both(f, k, h):
        for axis in range(2):
            f(k, h, axis)

    for h in hs:
        core_start(0, h)
    for h in hs:
        core_end(0, h)
    for h in hs:
        z_start(0, h)
    for h in hs:
        a_end(0, h)
    for h in hs:
        z_end(0, h)
        b_end(0, h)
    for k in range(STEPS - 1):
        for h in hs:
            gather_start(k, h)
        if k == 0:
            pick(1)
            e_core_start(1)
        both(ring_start, k, 0)
        both(ring_pass, k, 0)
        both(ring_start, k, 1)
        e_z_start(k + 1)
        if k == 0:
            pick(2)
            e_core_start(2)
        both(ring_end, k, 0)
        product(k + 1, 0)
        core_start(k + 1, 0)
        both(ring_pass, k, 1)
        core_end(k + 1, 0)
        z_start(k + 1, 0)
        both(ring_end, k, 1)
        product(k + 1, 1)
        core_start(k + 1, 1)
        a_end(k + 1, 0)
        core_end(k + 1, 1)
        z_end(k + 1, 0)
        z_start(k + 1, 1)
        a_end(k + 1, 1)
        b_end(k + 1, 0)
        z_end(k + 1, 1)
        b_end(k + 1, 1)

    parts = []
    for h in hs:
        v = lsum[h, 0:1, :]
        parts.append(jnp.where(zh == 0, v[:, 0:R], v[:, 64 : 64 + R]))
    logs[...] = parts[0] if HALVES == 1 else jnp.concatenate(parts, axis=1)

    for cp in drain:
        cp.wait_send()

    @pl.when(jnp.logical_not(is_self))
    def _():
        for k in range(STEPS - 1):
            for h in hs:
                st["near", k, h].wait_send()


def per_device(forward_init, transition, emission, tokens):
    hbm = pl.BlockSpec(memory_space=pl.ANY)
    vmem = pl.BlockSpec(memory_space=pltpu.VMEM)
    V = pltpu.VMEM
    D = pltpu.SemaphoreType.DMA
    f32, bf16 = jnp.float32, jnp.bfloat16
    H = HALVES
    out, logs = pl.pallas_call(
        kernel,
        name="forward_window",
        out_shape=(jax.ShapeDtypeStruct((64, BLK), f32), jax.ShapeDtypeStruct((1, 64), f32)),
        in_specs=[vmem, hbm, hbm, hbm],
        out_specs=(vmem, vmem),
        scratch_shapes=[
            V((KB, BLK, BLK), bf16),
            V((1024, BLK), bf16),
            V((KB, 256, BLK), f32),
            V((STEPS, KB, 256, BLK), bf16),
            V((STEPS, 256, BLK), f32),
            V((STEPS, H, 2 * R, BLK), f32),
            V((STEPS, H, 2 * R, BLK), f32),
            V((STEPS, H, R, BLK), f32),
            V((STEPS, 256, BLK), bf16),
            V((STEPS, 128, BLK), bf16),
            V((STEPS, H, 2 * R, BLK), bf16),
            V((STEPS, H, 2 * R, BLK), bf16),
            V((STEPS - 1, H, R, BLK), bf16),
            V((STEPS, H, 16, 8, 128), f32),
            V((STEPS, H, 4, 8, 128), f32),
            V((STEPS, H, R, BLK), f32),
            V((H, 8, 128), f32),
            V((H, 128, 128), f32),
            D((KB,)), D((KB,)), D,
            D((STEPS, H)), D((STEPS, H)), D((STEPS, H)), D((STEPS, H)),
            D((STEPS,)), D((STEPS,)), D((STEPS, H)), D((STEPS, H)),
            D((STEPS, H, 15)), D((STEPS, H)), D((STEPS, H, 3)), D((STEPS, H)),
            D((STEPS, H, 2)), D((STEPS, H)), D((STEPS, H, 2, 3)), D((STEPS, H, 2)),
            D((STEPS, H, 6)), D((STEPS, H, 6)), D((STEPS, H, 6)), D((STEPS, H, 6)),
        ],
        compiler_params=pltpu.CompilerParams(collective_id=0, has_side_effects=True, vmem_limit_bytes=60 * 2**20),
    )(tokens, forward_init, transition, emission)
    return out, logs.reshape(64)


def solution(mesh):
    placed = (P(None, "src"), P("src", "tgt"), P("src", "tgt"), P())
    return jax.shard_map(
        per_device,
        mesh=mesh,
        in_specs=placed,
        out_specs=(P("src", "tgt"), P("src")),
        check_vma=False,
    )
```

```python
import functools

import jax
import jax.numpy as jnp
from jax import lax
from jax.experimental import pallas as pl
from jax.experimental.pallas import tpu as pltpu
from jax.sharding import PartitionSpec as P

MESH = pl.DeviceIdType.MESH
BLK = 1024
KB = 8
HALVES = 2
R = 64 // HALVES
ROWS = 4 * R
CA = 512
STEPS = 3
AHEAD = 3
S = 32768.0


def place(q):
    return (q % 2) * 2 + q // 2


def kernel(tok, fwd, trans, emis, out, logs, tbuf, ebuf, stage, cur, acc, rs1, mid, rs2, erow, er1, emid, er2, blk, tota, totb, fresh, lsum, col,
           ld_t, ld_f, ld_e, d_s, d_r, z_s, z_r, ed_s, ed_r, ez_s, ez_r, a_s, a_r, b_s, b_r, t_s, t_r, g_s, g_r, xa_s, xa_r, yb_s, yb_r):
    s = lax.axis_index("src")
    t = lax.axis_index("tgt")
    zh, c = s // 2, s % 2
    y, zl, x = t // 8, (t // 4) % 2, t % 4
    is_self = s == y

    def dev(s_, y_, zl_, x_):
        return (s_, y_ * 8 + zl_ * 4 + x_)

    core = dev(zh * 2 + 1 - c, y, zl, x)
    zhp = dev((1 - zh) * 2 + c, y, zl, x)
    plane = [(dy, dx) for dy in range(4) for dx in range(4)][1:]
    line = [(dh, dz) for dh in range(2) for dz in range(2)][1:]

    def in_plane(dy, dx):
        return dev(s, (y + dy) % 4, zl, (x + dx) % 4)

    def in_z(dh, dz):
        return dev((zh + dh) % 2 * 2 + c, y, (zl + dz) % 2, x)

    def in_y(dy):
        return dev(s, (y + dy) % 4, zl, x)

    def in_x(dx):
        return dev(s, y, zl, (x + dx) % 4)

    def turned(dz):
        return dev(y, s, (zl + dz) % 2, x)

    def kb_rows(i):
        return pl.ds(pl.multiple_of(((i % 2) * 4 + i // 2) * BLK, BLK), BLK)

    def f_ld(i):
        return pltpu.make_async_copy(fwd.at[:, kb_rows(i)], stage.at[i], ld_f.at[i])

    def t_ld(i):
        return pltpu.make_async_copy(trans.at[kb_rows(i)], tbuf.at[i], ld_t.at[i])

    e_ld = pltpu.make_async_copy(emis, ebuf, ld_e)
    e_ld.start()

    barrier = pltpu.get_barrier_semaphore()

    def hello(d):
        pl.semaphore_signal(barrier, inc=1, device_id=d, device_id_type=MESH)

    hello(core)
    for p in plane:
        hello(in_plane(*p))
    for p in line:
        hello(in_z(*p))
    hello(turned(1))
    n = 1 + len(plane) + 3 + 1

    @pl.when(jnp.logical_not(is_self))
    def _():
        hello(turned(0))

    for i in range(AHEAD):
        f_ld(i).start()
        t_ld(i).start()

    def remote(src, dst, ss, rs, d):
        return pltpu.make_async_remote_copy(src_ref=src, dst_ref=dst, send_sem=ss, recv_sem=rs, device_id=d, device_id_type=MESH)

    drain = []

    def pick(k):
        ids = jnp.broadcast_to(tok[k : k + 1, :], (128, 256)).T - s * BLK
        ids = jnp.concatenate([ids[q * 64 : (q + 1) * 64, :] for q in (0, 2, 1, 3)], axis=0)
        lane = lax.broadcasted_iota(jnp.int32, (256, 128), 1)
        hot = jnp.concatenate([jnp.where(ids == lane + v * 128, 1.0, 0.0).astype(jnp.bfloat16) for v in range(8)], axis=1)
        erow[k] = jnp.dot(hot, ebuf[...], preferred_element_type=jnp.float32).astype(jnp.bfloat16)

    def own_rows(p, size):
        return pl.ds(pl.multiple_of(p * size, size), size)

    def part_rows(h, p, size):
        return pl.ds(pl.multiple_of(h * ROWS + p * size, size), size)

    est = {}

    def e_core_start(k):
        cp = remote(erow.at[k, own_rows(1 - c, 128)], er1.at[k], ed_s.at[k], ed_r.at[k], core)
        cp.start()
        est["d", k] = cp
        drain.append(cp)

    def e_z_start(k):
        est["d", k].wait_recv()
        for h in range(HALVES):
            for g in range(2):
                emid[k, h, g * R : (g + 1) * R, :] = erow[k, pl.ds(pl.multiple_of(c * 128 + g * 64 + h * R, R), R), :] + er1[k, g * 64 + h * R : g * 64 + (h + 1) * R, :]
            cp = remote(emid.at[k, h], er2.at[k, h], ez_s.at[k, h], ez_r.at[k, h], zhp)
            cp.start()
            est["z", k, h] = cp
            drain.append(cp)

    e_ld.wait()
    for i in range(AHEAD, KB):
        f_ld(i).start()
        t_ld(i).start()
    pick(0)

    @pl.when(is_self)
    def _():
        pl.semaphore_wait(barrier, n)

    @pl.when(jnp.logical_not(is_self))
    def _():
        pl.semaphore_wait(barrier, n + 1)

    e_core_start(0)
    e_z_start(0)

    acc[0] = jnp.zeros_like(acc[0])

    def first(i, _):
        f_ld(i).wait()
        for q in range(4):
            for h in range(HALVES):
                at = h * ROWS + place(q) * R
                cur[0, i, at : at + R, :] = stage[i, q * 64 + h * R : q * 64 + (h + 1) * R, :].astype(jnp.bfloat16)
        t_ld(i).wait()

        acc[0] += jnp.dot(cur[0, i], tbuf[i], preferred_element_type=jnp.float32)
        return 0

    lax.fori_loop(0, KB, first, 0)

    def product(k, h):
        def body(j, _):
            cols = pl.ds(pl.multiple_of(j * 512, 512), 512)
            v = jnp.dot(cur[k, 0, h * ROWS : (h + 1) * ROWS, :], tbuf[0, :, cols], preferred_element_type=jnp.float32)
            for i in range(1, KB):
                v = v + jnp.dot(cur[k, i, h * ROWS : (h + 1) * ROWS, :], tbuf[i, :, cols], preferred_element_type=jnp.float32)
            acc[k, h * ROWS : (h + 1) * ROWS, cols] = v
            return 0

        lax.fori_loop(0, BLK // 512, body, 0)

    def product_early(k, h):
        rows = slice(h * ROWS, (h + 1) * ROWS)

        def body(j, _):
            cols = pl.ds(pl.multiple_of(j * 512, 512), 512)
            v = jnp.zeros((ROWS, 512), jnp.float32)
            for d in (0, 1, 3):
                for z in range(2):
                    i = (x + d) % 4 * 2 + z
                    v = v + jnp.dot(cur[k, i, rows, 0:CA], tbuf[i, 0:CA, cols], preferred_element_type=jnp.float32)
            acc[k, rows, cols] = v
            return 0

        lax.fori_loop(0, BLK // 512, body, 0)

    def product_late(k, h):
        rows = slice(h * ROWS, (h + 1) * ROWS)

        def body(j, _):
            cols = pl.ds(pl.multiple_of(j * 512, 512), 512)
            v = acc[k, rows, cols]
            for z in range(2):
                i = (x + 2) % 4 * 2 + z
                v = v + jnp.dot(cur[k, i, rows, 0:CA], tbuf[i, 0:CA, cols], preferred_element_type=jnp.float32)
            for i in range(KB):
                v = v + jnp.dot(cur[k, i, rows, CA:BLK], tbuf[i, CA:BLK, cols], preferred_element_type=jnp.float32)
            acc[k, rows, cols] = v
            return 0

        lax.fori_loop(0, BLK // 512, body, 0)

    st = {}

    def core_start(k, h):
        cp = remote(acc.at[k, part_rows(h, 1 - c, 2 * R)], rs1.at[k, h], d_s.at[k, h], d_r.at[k, h], core)
        cp.start()
        st["d", k, h] = cp
        drain.append(cp)

    def emission(k, h, g):
        rows = own_rows(g, R)
        return emid[k, h, rows, :].astype(jnp.float32) + er2[k, h, rows, :].astype(jnp.float32)

    def core_end(k, h):
        st["d", k, h].wait_recv()
        mid[k, h] = acc[k, part_rows(h, c, 2 * R), :] + rs1[k, h]
        z_start(k, h)

    def share(k, h):
        est["z", k, h].wait_recv()
        parts = []
        for g in range(2):
            v = mid[k, h, g * R : (g + 1) * R, :] * emission(k, h, g)
            lanes = v[:, 0:128]
            for j in range(1, 8):
                lanes = lanes + v[:, j * 128 : (j + 1) * 128]
            parts.append(lanes)
            if R < 64:
                parts.append(jnp.zeros((64 - R, 128), jnp.float32))
        sums = jnp.sum(jnp.concatenate(parts, axis=0).T, axis=0, keepdims=True)
        own = y * 4 + x
        tota[k, h, own] = jnp.broadcast_to(sums, (8, 128))
        for j, p in enumerate(plane):
            cp = remote(tota.at[k, h, own], tota.at[k, h, own], a_s.at[k, h, j], a_r.at[k, h], in_plane(*p))
            cp.start()
            drain.append(cp)

    def z_start(k, h):
        cp = remote(mid.at[k, h, own_rows(1 - zh, R)], rs2.at[k, h], z_s.at[k, h], z_r.at[k, h], zhp)
        cp.start()
        st["z", k, h] = cp
        drain.append(cp)

    def a_end(k, h):
        pltpu.make_async_copy(tota.at[k, h, pl.ds(0, 15)], tota.at[k, h, pl.ds(0, 15)], a_r.at[k, h]).wait()
        v = tota[k, h, 0]
        for j in range(1, 16):
            v = v + tota[k, h, j]
        own = zh * 2 + zl
        totb[k, h, own] = v
        for j, p in enumerate(line):
            cp = remote(totb.at[k, h, own], totb.at[k, h, own], b_s.at[k, h, j], b_r.at[k, h], in_z(*p))
            cp.start()
            drain.append(cp)

    def z_end(k, h):
        st["z", k, h].wait_recv()
        fresh[k, h] = (mid[k, h, own_rows(zh, R), :] + rs2[k, h]) * emission(k, h, zh) * (1.0 / S)

    def b_end(k, h):
        pltpu.make_async_copy(totb.at[k, h, pl.ds(0, 3)], totb.at[k, h, pl.ds(0, 3)], b_r.at[k, h]).wait()
        v = totb[k, h, 0]
        for j in range(1, 4):
            v = v + totb[k, h, j]
        total = v * (1.0 / (S * S))
        col[h] = jnp.broadcast_to(total[0:1, :], (128, 128)).T
        normed = fresh[k, h] / col[h, pl.ds(pl.multiple_of(zh * 64, 64), R), 0:1]
        if k + 1 == STEPS:
            out[h * R : (h + 1) * R, :] = normed
        else:
            blk[k, h] = normed.astype(jnp.bfloat16)
            dst = cur.at[k + 1, x * 2 + zl, part_rows(h, place(s), R)]
            far = remote(blk.at[k, h], dst, t_s.at[k, h, 1], t_r.at[k, h], turned(1))
            far.start()
            drain.append(far)
            near = remote(blk.at[k, h], dst, t_s.at[k, h, 0], t_r.at[k, h], turned(0))
            here = pltpu.make_async_copy(blk.at[k, h], dst, t_r.at[k, h])

            @pl.when(is_self)
            def _():
                here.start()

            @pl.when(jnp.logical_not(is_self))
            def _():
                near.start()

            st["near", k, h] = near
        lsum[h] = jnp.log(total) if k == 0 else lsum[h] + jnp.log(total)

    def gather_start(k, h):
        rows = part_rows(h, place(y), R)
        whole = cur.at[k + 1, pl.ds(x * 2, 2), rows]
        pltpu.make_async_copy(whole, whole, t_r.at[k, h]).wait()
        for j in (0, 2, 1):
            for axis, cols, d in ((0, pl.ds(0, CA), in_y(j + 1)), (1, pl.ds(CA, BLK - CA), in_x(j + 1))):
                p = cur.at[k + 1, pl.ds(x * 2, 2), rows, cols]
                cp = remote(p, p, g_s.at[k, h, axis, j], g_r.at[k, h, axis], d)
                cp.start()
                drain.append(cp)

    def piece_a(k, h, xx, z):
        return cur.at[k + 1, xx * 2 + z, pl.ds(h * ROWS, ROWS), pl.ds(0, CA)]

    def piece_b(k, h, yy, z):
        return cur.at[k + 1, pl.ds(z * 4, 4), part_rows(h, place(yy), R), pl.ds(CA, BLK - CA)]

    def ring_dev(axis, d):
        return in_x(d + 4) if axis == 0 else in_y(d + 4)

    def ring_start(k, h, axis):
        if axis == 0:
            got = cur.at[k + 1, pl.ds(x * 2, 2), pl.ds(h * ROWS, 3 * R), pl.ds(0, CA)]
        else:
            got = cur.at[k + 1, pl.ds(0, 6), part_rows(h, place(y), R), pl.ds(CA, BLK - CA)]
        pltpu.make_async_copy(got, got, g_r.at[k, h, axis]).wait()
        piece, me = (piece_a, x) if axis == 0 else (piece_b, y)
        ss, rs = (xa_s, xa_r) if axis == 0 else (yb_s, yb_r)
        for j, (d, z) in enumerate(((1, 0), (-1, 1), (1, 1), (-1, 0))):
            p = piece(k, h, me, z)
            cp = remote(p, p, ss.at[k, h, j], rs.at[k, h, j], ring_dev(axis, d))
            cp.start()
            st["r", k, h, axis, j] = cp
            drain.append(cp)

    def ring_pass(k, h, axis):
        piece, me = (piece_a, x) if axis == 0 else (piece_b, y)
        ss, rs = (xa_s, xa_r) if axis == 0 else (yb_s, yb_r)
        for j, (d, z) in ((0, (1, 0)), (1, (-1, 1))):
            st["r", k, h, axis, j].wait_recv()
            p = piece(k, h, (me - d + 4) % 4, z)
            cp = remote(p, p, ss.at[k, h, 4 + j], rs.at[k, h, 4 + j], ring_dev(axis, d))
            cp.start()
            st["r", k, h, axis, 4 + j] = cp
            drain.append(cp)

    def ring_end(k, h, axis):
        for j in range(2, 6):
            st["r", k, h, axis, j].wait_recv()

    hs = range(HALVES)

    def both(f, k, h):
        for axis in range(2):
            f(k, h, axis)

    for h in hs:
        core_start(0, h)
    for h in hs:
        core_end(0, h)
    for h in hs:
        share(0, h)
    for h in hs:
        a_end(0, h)
    for h in hs:
        z_end(0, h)
        b_end(0, h)
    for k in range(STEPS - 1):
        for h in hs:
            gather_start(k, h)
        if k == 0:
            pick(1)
            e_core_start(1)
        both(ring_start, k, 0)
        if k == 0:
            e_z_start(1)
        both(ring_pass, k, 0)
        both(ring_start, k, 1)
        if k == 0:
            pick(2)
            e_core_start(2)
            e_z_start(2)
        both(ring_end, k, 0)
        product(k + 1, 0)
        core_start(k + 1, 0)
        both(ring_pass, k, 1)
        core_end(k + 1, 0)
        share(k + 1, 0)
        for j in (2, 3):
            st["r", k, 1, 0, j].wait_recv()
        product_early(k + 1, 1)
        for j in (4, 5):
            st["r", k, 1, 0, j].wait_recv()
        ring_end(k, 1, 1)
        product_late(k + 1, 1)
        core_start(k + 1, 1)
        a_end(k + 1, 0)
        core_end(k + 1, 1)
        share(k + 1, 1)
        z_end(k + 1, 0)
        a_end(k + 1, 1)
        b_end(k + 1, 0)
        z_end(k + 1, 1)
        b_end(k + 1, 1)

    parts = []
    for h in hs:
        v = lsum[h, 0:1, :]
        parts.append(jnp.where(zh == 0, v[:, 0:R], v[:, 64 : 64 + R]))
    logs[...] = parts[0] if HALVES == 1 else jnp.concatenate(parts, axis=1)

    for cp in drain:
        cp.wait_send()

    @pl.when(jnp.logical_not(is_self))
    def _():
        for k in range(STEPS - 1):
            for h in hs:
                st["near", k, h].wait_send()


def per_device(forward_init, transition, emission, tokens):
    hbm = pl.BlockSpec(memory_space=pl.ANY)
    vmem = pl.BlockSpec(memory_space=pltpu.VMEM)
    V = pltpu.VMEM
    D = pltpu.SemaphoreType.DMA
    f32, bf16 = jnp.float32, jnp.bfloat16
    H = HALVES
    out, logs = pl.pallas_call(
        kernel,
        name="forward_window",
        out_shape=(jax.ShapeDtypeStruct((64, BLK), f32), jax.ShapeDtypeStruct((1, 64), f32)),
        in_specs=[vmem, hbm, hbm, hbm],
        out_specs=(vmem, vmem),
        scratch_shapes=[
            V((KB, BLK, BLK), bf16),
            V((1024, BLK), bf16),
            V((KB, 256, BLK), f32),
            V((STEPS, KB, 256, BLK), bf16),
            V((STEPS, 256, BLK), f32),
            V((STEPS, H, 2 * R, BLK), f32),
            V((STEPS, H, 2 * R, BLK), f32),
            V((STEPS, H, R, BLK), f32),
            V((STEPS, 256, BLK), bf16),
            V((STEPS, 128, BLK), bf16),
            V((STEPS, H, 2 * R, BLK), bf16),
            V((STEPS, H, 2 * R, BLK), bf16),
            V((STEPS - 1, H, R, BLK), bf16),
            V((STEPS, H, 16, 8, 128), f32),
            V((STEPS, H, 4, 8, 128), f32),
            V((STEPS, H, R, BLK), f32),
            V((H, 8, 128), f32),
            V((H, 128, 128), f32),
            D((KB,)), D((KB,)), D,
            D((STEPS, H)), D((STEPS, H)), D((STEPS, H)), D((STEPS, H)),
            D((STEPS,)), D((STEPS,)), D((STEPS, H)), D((STEPS, H)),
            D((STEPS, H, 15)), D((STEPS, H)), D((STEPS, H, 3)), D((STEPS, H)),
            D((STEPS, H, 2)), D((STEPS, H)), D((STEPS, H, 2, 3)), D((STEPS, H, 2)),
            D((STEPS, H, 6)), D((STEPS, H, 6)), D((STEPS, H, 6)), D((STEPS, H, 6)),
        ],
        compiler_params=pltpu.CompilerParams(collective_id=0, has_side_effects=True, vmem_limit_bytes=60 * 2**20),
    )(tokens, forward_init, transition, emission)
    return out, logs.reshape(64)


def solution(mesh):
    placed = (P(None, "src"), P("src", "tgt"), P("src", "tgt"), P())
    return jax.shard_map(
        per_device,
        mesh=mesh,
        in_specs=placed,
        out_specs=(P("src", "tgt"), P("src")),
        check_vma=False,
    )
```

```python
import functools

import jax
import jax.numpy as jnp
from jax import lax
from jax.experimental import pallas as pl
from jax.experimental.pallas import tpu as pltpu
from jax.sharding import PartitionSpec as P

MESH = pl.DeviceIdType.MESH
BLK = 1024
KB = 8
HALVES = 2
R = 64 // HALVES
ROWS = 4 * R
CA = 512
STEPS = 3
AHEAD = 3
S = 32768.0


def place(q):
    return (q % 2) * 2 + q // 2


def kernel(toks, fwd, trans, emis, outs, logs, tok, out, ld_k, o_s, tbuf, ebuf, stage, cur, acc, rs1, mid, rs2, erow, er1, emid, er2, blk, tota, totb, fresh, lsum, col,
           ld_t, ld_f, ld_e, d_s, d_r, z_s, z_r, ed_s, ed_r, ez_s, ez_r, a_s, a_r, b_s, b_r, t_s, t_r, g_s, g_r, xa_s, xa_r, yb_s, yb_r):
    s = lax.axis_index("src")
    t = lax.axis_index("tgt")
    zh, c = s // 2, s % 2
    y, zl, x = t // 8, (t // 4) % 2, t % 4
    is_self = s == y

    def dev(s_, y_, zl_, x_):
        return (s_, y_ * 8 + zl_ * 4 + x_)

    core = dev(zh * 2 + 1 - c, y, zl, x)
    zhp = dev((1 - zh) * 2 + c, y, zl, x)
    plane = [(dy, dx) for dy in range(4) for dx in range(4)][1:]
    line = [(dh, dz) for dh in range(2) for dz in range(2)][1:]

    def in_plane(dy, dx):
        return dev(s, (y + dy) % 4, zl, (x + dx) % 4)

    def in_z(dh, dz):
        return dev((zh + dh) % 2 * 2 + c, y, (zl + dz) % 2, x)

    def in_y(dy):
        return dev(s, (y + dy) % 4, zl, x)

    def in_x(dx):
        return dev(s, y, zl, (x + dx) % 4)

    def turned(dz):
        return dev(y, s, (zl + dz) % 2, x)

    def kb_rows(i):
        return pl.ds(pl.multiple_of(((i % 2) * 4 + i // 2) * BLK, BLK), BLK)

    def f_ld(i):
        return pltpu.make_async_copy(fwd.at[:, kb_rows(i)], stage.at[i], ld_f.at[i])

    def t_ld(i):
        return pltpu.make_async_copy(trans.at[kb_rows(i)], tbuf.at[i], ld_t.at[i])

    e_ld = pltpu.make_async_copy(emis, ebuf, ld_e)
    e_ld.start()
    k_ld = pltpu.make_async_copy(toks, tok, ld_k)
    k_ld.start()

    barrier = pltpu.get_barrier_semaphore()

    def hello(d):
        pl.semaphore_signal(barrier, inc=1, device_id=d, device_id_type=MESH)

    hello(core)
    for p in plane:
        hello(in_plane(*p))
    for p in line:
        hello(in_z(*p))
    hello(turned(1))
    n = 1 + len(plane) + 3 + 1

    @pl.when(jnp.logical_not(is_self))
    def _():
        hello(turned(0))

    for i in range(AHEAD):
        f_ld(i).start()
        t_ld(i).start()

    def remote(src, dst, ss, rs, d):
        return pltpu.make_async_remote_copy(src_ref=src, dst_ref=dst, send_sem=ss, recv_sem=rs, device_id=d, device_id_type=MESH)

    drain = []

    def pick(k):
        ids = jnp.broadcast_to(tok[k : k + 1, :], (128, 256)).T - s * BLK
        ids = jnp.concatenate([ids[q * 64 : (q + 1) * 64, :] for q in (0, 2, 1, 3)], axis=0)
        lane = lax.broadcasted_iota(jnp.int32, (256, 128), 1)
        hot = jnp.concatenate([jnp.where(ids == lane + v * 128, 1.0, 0.0).astype(jnp.bfloat16) for v in range(8)], axis=1)
        erow[k] = jnp.dot(hot, ebuf[...], preferred_element_type=jnp.float32).astype(jnp.bfloat16)

    def own_rows(p, size):
        return pl.ds(pl.multiple_of(p * size, size), size)

    def part_rows(h, p, size):
        return pl.ds(pl.multiple_of(h * ROWS + p * size, size), size)

    est = {}

    def e_core_start(k):
        cp = remote(erow.at[k, own_rows(1 - c, 128)], er1.at[k], ed_s.at[k], ed_r.at[k], core)
        cp.start()
        est["d", k] = cp
        drain.append(cp)

    def e_z_start(k):
        est["d", k].wait_recv()
        for h in range(HALVES):
            for g in range(2):
                emid[k, h, g * R : (g + 1) * R, :] = erow[k, pl.ds(pl.multiple_of(c * 128 + g * 64 + h * R, R), R), :] + er1[k, g * 64 + h * R : g * 64 + (h + 1) * R, :]
            cp = remote(emid.at[k, h], er2.at[k, h], ez_s.at[k, h], ez_r.at[k, h], zhp)
            cp.start()
            est["z", k, h] = cp
            drain.append(cp)

    k_ld.wait()
    e_ld.wait()
    for i in range(AHEAD, KB):
        f_ld(i).start()
        t_ld(i).start()
    pick(0)

    @pl.when(is_self)
    def _():
        pl.semaphore_wait(barrier, n)

    @pl.when(jnp.logical_not(is_self))
    def _():
        pl.semaphore_wait(barrier, n + 1)

    e_core_start(0)
    e_z_start(0)

    acc[0] = jnp.zeros_like(acc[0])

    def first(i, _):
        f_ld(i).wait()
        for q in range(4):
            for h in range(HALVES):
                at = h * ROWS + place(q) * R
                cur[0, i, at : at + R, :] = stage[i, q * 64 + h * R : q * 64 + (h + 1) * R, :].astype(jnp.bfloat16)
        t_ld(i).wait()

        acc[0] += jnp.dot(cur[0, i], tbuf[i], preferred_element_type=jnp.float32)
        return 0

    lax.fori_loop(0, KB, first, 0)

    def product(k, h):
        def body(j, _):
            cols = pl.ds(pl.multiple_of(j * 512, 512), 512)
            v = jnp.dot(cur[k, 0, h * ROWS : (h + 1) * ROWS, :], tbuf[0, :, cols], preferred_element_type=jnp.float32)
            for i in range(1, KB):
                v = v + jnp.dot(cur[k, i, h * ROWS : (h + 1) * ROWS, :], tbuf[i, :, cols], preferred_element_type=jnp.float32)
            acc[k, h * ROWS : (h + 1) * ROWS, cols] = v
            return 0

        lax.fori_loop(0, BLK // 512, body, 0)

    def product_early(k, h):
        rows = slice(h * ROWS, (h + 1) * ROWS)

        def body(j, _):
            cols = pl.ds(pl.multiple_of(j * 512, 512), 512)
            v = jnp.zeros((ROWS, 512), jnp.float32)
            for d in (0, 1, 3):
                for z in range(2):
                    i = (x + d) % 4 * 2 + z
                    v = v + jnp.dot(cur[k, i, rows, 0:CA], tbuf[i, 0:CA, cols], preferred_element_type=jnp.float32)
            acc[k, rows, cols] = v
            return 0

        lax.fori_loop(0, BLK // 512, body, 0)

    def product_late(k, h):
        rows = slice(h * ROWS, (h + 1) * ROWS)

        def body(j, _):
            cols = pl.ds(pl.multiple_of(j * 512, 512), 512)
            v = acc[k, rows, cols]
            for z in range(2):
                i = (x + 2) % 4 * 2 + z
                v = v + jnp.dot(cur[k, i, rows, 0:CA], tbuf[i, 0:CA, cols], preferred_element_type=jnp.float32)
            for i in range(KB):
                v = v + jnp.dot(cur[k, i, rows, CA:BLK], tbuf[i, CA:BLK, cols], preferred_element_type=jnp.float32)
            acc[k, rows, cols] = v
            return 0

        lax.fori_loop(0, BLK // 512, body, 0)

    st = {}

    def core_start(k, h):
        cp = remote(acc.at[k, part_rows(h, 1 - c, 2 * R)], rs1.at[k, h], d_s.at[k, h], d_r.at[k, h], core)
        cp.start()
        st["d", k, h] = cp
        drain.append(cp)

    def emission(k, h, g):
        rows = own_rows(g, R)
        return emid[k, h, rows, :].astype(jnp.float32) + er2[k, h, rows, :].astype(jnp.float32)

    def core_end(k, h):
        st["d", k, h].wait_recv()
        mid[k, h] = acc[k, part_rows(h, c, 2 * R), :] + rs1[k, h]
        z_start(k, h)

    def share(k, h):
        est["z", k, h].wait_recv()
        parts = []
        for g in range(2):
            v = mid[k, h, g * R : (g + 1) * R, :] * emission(k, h, g)
            lanes = v[:, 0:128]
            for j in range(1, 8):
                lanes = lanes + v[:, j * 128 : (j + 1) * 128]
            parts.append(lanes)
            if R < 64:
                parts.append(jnp.zeros((64 - R, 128), jnp.float32))
        sums = jnp.sum(jnp.concatenate(parts, axis=0).T, axis=0, keepdims=True)
        own = y * 4 + x
        tota[k, h, own] = jnp.broadcast_to(sums, (8, 128))
        for j, p in enumerate(plane):
            cp = remote(tota.at[k, h, own], tota.at[k, h, own], a_s.at[k, h, j], a_r.at[k, h], in_plane(*p))
            cp.start()
            drain.append(cp)

    def z_start(k, h):
        cp = remote(mid.at[k, h, own_rows(1 - zh, R)], rs2.at[k, h], z_s.at[k, h], z_r.at[k, h], zhp)
        cp.start()
        st["z", k, h] = cp
        drain.append(cp)

    def a_end(k, h):
        pltpu.make_async_copy(tota.at[k, h, pl.ds(0, 15)], tota.at[k, h, pl.ds(0, 15)], a_r.at[k, h]).wait()
        v = tota[k, h, 0]
        for j in range(1, 16):
            v = v + tota[k, h, j]
        own = zh * 2 + zl
        totb[k, h, own] = v
        for j, p in enumerate(line):
            cp = remote(totb.at[k, h, own], totb.at[k, h, own], b_s.at[k, h, j], b_r.at[k, h], in_z(*p))
            cp.start()
            drain.append(cp)

    def z_end(k, h):
        st["z", k, h].wait_recv()
        fresh[k, h] = (mid[k, h, own_rows(zh, R), :] + rs2[k, h]) * emission(k, h, zh) * (1.0 / S)

    def b_end(k, h):
        pltpu.make_async_copy(totb.at[k, h, pl.ds(0, 3)], totb.at[k, h, pl.ds(0, 3)], b_r.at[k, h]).wait()
        v = totb[k, h, 0]
        for j in range(1, 4):
            v = v + totb[k, h, j]
        total = v * (1.0 / (S * S))
        col[h] = jnp.broadcast_to(total[0:1, :], (128, 128)).T
        normed = fresh[k, h] / col[h, pl.ds(pl.multiple_of(zh * 64, 64), R), 0:1]
        if k + 1 == STEPS:
            out[h * R : (h + 1) * R, :] = normed
            pltpu.make_async_copy(out.at[pl.ds(h * R, R)], outs.at[pl.ds(h * R, R)], o_s.at[h]).start()
        else:
            blk[k, h] = normed.astype(jnp.bfloat16)
            dst = cur.at[k + 1, x * 2 + zl, part_rows(h, place(s), R)]
            far = remote(blk.at[k, h], dst, t_s.at[k, h, 1], t_r.at[k, h], turned(1))
            far.start()
            drain.append(far)
            near = remote(blk.at[k, h], dst, t_s.at[k, h, 0], t_r.at[k, h], turned(0))
            here = pltpu.make_async_copy(blk.at[k, h], dst, t_r.at[k, h])

            @pl.when(is_self)
            def _():
                here.start()

            @pl.when(jnp.logical_not(is_self))
            def _():
                near.start()

            st["near", k, h] = near
        lsum[h] = jnp.log(total) if k == 0 else lsum[h] + jnp.log(total)

    def gather_start(k, h):
        rows = part_rows(h, place(y), R)
        whole = cur.at[k + 1, pl.ds(x * 2, 2), rows]
        pltpu.make_async_copy(whole, whole, t_r.at[k, h]).wait()
        for j in (0, 2, 1):
            for axis, cols, d in ((0, pl.ds(0, CA), in_y(j + 1)), (1, pl.ds(CA, BLK - CA), in_x(j + 1))):
                p = cur.at[k + 1, pl.ds(x * 2, 2), rows, cols]
                cp = remote(p, p, g_s.at[k, h, axis, j], g_r.at[k, h, axis], d)
                cp.start()
                drain.append(cp)

    def piece_a(k, h, xx, z):
        return cur.at[k + 1, xx * 2 + z, pl.ds(h * ROWS, ROWS), pl.ds(0, CA)]

    def piece_b(k, h, yy, z):
        return cur.at[k + 1, pl.ds(z * 4, 4), part_rows(h, place(yy), R), pl.ds(CA, BLK - CA)]

    def ring_dev(axis, d):
        return in_x(d + 4) if axis == 0 else in_y(d + 4)

    def ring_start(k, h, axis):
        if axis == 0:
            got = cur.at[k + 1, pl.ds(x * 2, 2), pl.ds(h * ROWS, 3 * R), pl.ds(0, CA)]
        else:
            got = cur.at[k + 1, pl.ds(0, 6), part_rows(h, place(y), R), pl.ds(CA, BLK - CA)]
        pltpu.make_async_copy(got, got, g_r.at[k, h, axis]).wait()
        piece, me = (piece_a, x) if axis == 0 else (piece_b, y)
        ss, rs = (xa_s, xa_r) if axis == 0 else (yb_s, yb_r)
        for j, (d, z) in enumerate(((1, 0), (-1, 1), (1, 1), (-1, 0))):
            p = piece(k, h, me, z)
            cp = remote(p, p, ss.at[k, h, j], rs.at[k, h, j], ring_dev(axis, d))
            cp.start()
            st["r", k, h, axis, j] = cp
            drain.append(cp)

    def ring_pass(k, h, axis):
        piece, me = (piece_a, x) if axis == 0 else (piece_b, y)
        ss, rs = (xa_s, xa_r) if axis == 0 else (yb_s, yb_r)
        for j, (d, z) in ((0, (1, 0)), (1, (-1, 1))):
            st["r", k, h, axis, j].wait_recv()
            p = piece(k, h, (me - d + 4) % 4, z)
            cp = remote(p, p, ss.at[k, h, 4 + j], rs.at[k, h, 4 + j], ring_dev(axis, d))
            cp.start()
            st["r", k, h, axis, 4 + j] = cp
            drain.append(cp)

    def ring_end(k, h, axis):
        for j in range(2, 6):
            st["r", k, h, axis, j].wait_recv()

    hs = range(HALVES)

    def both(f, k, h):
        for axis in range(2):
            f(k, h, axis)

    for h in hs:
        core_start(0, h)
    for h in hs:
        core_end(0, h)
    for h in hs:
        share(0, h)
    for h in hs:
        a_end(0, h)
    for h in hs:
        z_end(0, h)
        b_end(0, h)
    for k in range(STEPS - 1):
        for h in hs:
            gather_start(k, h)
        if k == 0:
            pick(1)
            e_core_start(1)
        both(ring_start, k, 0)
        if k == 0:
            e_z_start(1)
        both(ring_pass, k, 0)
        both(ring_start, k, 1)
        if k == 0:
            pick(2)
            e_core_start(2)
            e_z_start(2)
        both(ring_end, k, 0)
        product(k + 1, 0)
        core_start(k + 1, 0)
        both(ring_pass, k, 1)
        core_end(k + 1, 0)
        share(k + 1, 0)
        for j in (2, 3):
            st["r", k, 1, 0, j].wait_recv()
        product_early(k + 1, 1)
        for j in (4, 5):
            st["r", k, 1, 0, j].wait_recv()
        ring_end(k, 1, 1)
        product_late(k + 1, 1)
        core_start(k + 1, 1)
        a_end(k + 1, 0)
        core_end(k + 1, 1)
        share(k + 1, 1)
        z_end(k + 1, 0)
        a_end(k + 1, 1)
        b_end(k + 1, 0)
        z_end(k + 1, 1)
        b_end(k + 1, 1)

    parts = []
    for h in hs:
        v = lsum[h, 0:1, :]
        parts.append(jnp.where(zh == 0, v[:, 0:R], v[:, 64 : 64 + R]))
    logs[...] = parts[0] if HALVES == 1 else jnp.concatenate(parts, axis=1)

    for cp in drain:
        cp.wait_send()
    for h in hs:
        pltpu.make_async_copy(out.at[pl.ds(h * R, R)], outs.at[pl.ds(h * R, R)], o_s.at[h]).wait()

    @pl.when(jnp.logical_not(is_self))
    def _():
        for k in range(STEPS - 1):
            for h in hs:
                st["near", k, h].wait_send()


def per_device(forward_init, transition, emission, tokens):
    hbm = pl.BlockSpec(memory_space=pl.ANY)
    vmem = pl.BlockSpec(memory_space=pltpu.VMEM)
    V = pltpu.VMEM
    D = pltpu.SemaphoreType.DMA
    f32, bf16 = jnp.float32, jnp.bfloat16
    H = HALVES
    out, logs = pl.pallas_call(
        kernel,
        name="forward_window",
        out_shape=(jax.ShapeDtypeStruct((64, BLK), f32), jax.ShapeDtypeStruct((1, 64), f32)),
        in_specs=[hbm, hbm, hbm, hbm],
        out_specs=(hbm, vmem),
        scratch_shapes=[
            V((STEPS, 256), jnp.int32),
            V((64, BLK), f32),
            D, D((H,)),
            V((KB, BLK, BLK), bf16),
            V((1024, BLK), bf16),
            V((KB, 256, BLK), f32),
            V((STEPS, KB, 256, BLK), bf16),
            V((STEPS, 256, BLK), f32),
            V((STEPS, H, 2 * R, BLK), f32),
            V((STEPS, H, 2 * R, BLK), f32),
            V((STEPS, H, R, BLK), f32),
            V((STEPS, 256, BLK), bf16),
            V((STEPS, 128, BLK), bf16),
            V((STEPS, H, 2 * R, BLK), bf16),
            V((STEPS, H, 2 * R, BLK), bf16),
            V((STEPS - 1, H, R, BLK), bf16),
            V((STEPS, H, 16, 8, 128), f32),
            V((STEPS, H, 4, 8, 128), f32),
            V((STEPS, H, R, BLK), f32),
            V((H, 8, 128), f32),
            V((H, 128, 128), f32),
            D((KB,)), D((KB,)), D,
            D((STEPS, H)), D((STEPS, H)), D((STEPS, H)), D((STEPS, H)),
            D((STEPS,)), D((STEPS,)), D((STEPS, H)), D((STEPS, H)),
            D((STEPS, H, 15)), D((STEPS, H)), D((STEPS, H, 3)), D((STEPS, H)),
            D((STEPS, H, 2)), D((STEPS, H)), D((STEPS, H, 2, 3)), D((STEPS, H, 2)),
            D((STEPS, H, 6)), D((STEPS, H, 6)), D((STEPS, H, 6)), D((STEPS, H, 6)),
        ],
        compiler_params=pltpu.CompilerParams(collective_id=0, has_side_effects=True, vmem_limit_bytes=60 * 2**20),
    )(tokens, forward_init, transition, emission)
    return out, logs.reshape(64)


def solution(mesh):
    placed = (P(None, "src"), P("src", "tgt"), P("src", "tgt"), P())
    return jax.shard_map(
        per_device,
        mesh=mesh,
        in_specs=placed,
        out_specs=(P("src", "tgt"), P("src")),
        check_vma=False,
    )
```
